256 devices in a mesh: sample: 8 (over y, core), slab: 32 (over x, z).
Axes of the slice: x: 4, y: 4, z: 8, core: 2. Of those that a mesh axis runs over, the one named last changes fastest.
Arguments:
- volume: bfloat16 [8, 32, 32, 32, 128], P('sample', 'slab'), may hold values from -6 to 6
- kernel: bfloat16 [27, 128, 128], replicated, may hold values from -0.109375 to 0.109375
- cotangent: bfloat16 [8, 32, 32, 32, 128], P('sample', 'slab'), may hold values from -6 to 6
Outputs:
- response: bfloat16 [8, 32, 32, 32, 128], P('sample', 'slab')
- grad_volume: bfloat16 [8, 32, 32, 32, 128], P('sample', 'slab')
- grad_kernel: float32 [128, 27, 128], P('slab')
The draws below stay inside these ranges and needn't reach their ends.
All inputs are finite; a program needn't handle non-finite values.
Results may differ from the reference program's by a relative error of at most 0.001.
Values may be sent and summed in bfloat16 or wider, within the bound.
No kernel may reach another device: no remote copies, remote signals or barrier semaphores. Data moves between devices by JAX's collectives and lax.ppermute only.
A program may use at most 64 MiB of HBM per device.

```python
import math
import jax
import jax.numpy as jnp
from jax import lax

C = 128
GRID = 32
SAMPLES = 8
Z = 32


def raised(drawn, rng, source, target, blocks, factor):
    def block_of(dim):
        return (jnp.arange(drawn.shape[dim]) // (drawn.shape[dim] // blocks)).reshape((-1,) + (1,) * (drawn.ndim - 1 - dim))

    near = jax.random.permutation(rng, blocks)[block_of(target)]
    second = (block_of(target) + blocks // 2) % blocks
    return jnp.where((block_of(source) == near) | (block_of(source) == second), factor * drawn, drawn)


def level_of(rng, dims, split, least, high):
    level = 1.0
    for dim, shards_of in split:
        heights = jax.random.uniform(jax.random.fold_in(jax.random.fold_in(rng, 6), dim), (shards_of,), jnp.float32, least / len(split), high / len(split))
        level = level * jnp.repeat(jnp.exp(heights), dims[dim] // shards_of).reshape((-1,) + (1,) * (len(dims) - 1 - dim))
    return level


def scatter_about(own_key, extent, width, most, pieces=(), held_as=jnp.bfloat16):
    loudness = level_of(own_key, extent, pieces, -0.22, 0.18) if pieces else 1.0
    result = jax.random.normal(own_key, extent, jnp.float32) * width * loudness
    return jnp.minimum(jnp.maximum(result, -most), most).astype(held_as)


def heavy_noise(own_key, extent, deviation, most, split, heavy, held_as=jnp.bfloat16):
    values = deviation * jax.random.normal(own_key, extent, jnp.float32)
    if split:
        values = values * level_of(own_key, extent, split, -0.22, 0.18)
    return jnp.clip(raised(values, jax.random.fold_in(own_key, 3), *heavy), -most, most).astype(held_as)


def setup_inputs(seed: int = 0) -> dict:
    splits = jax.random.split(jax.random.key(seed), 4)
    volume = scatter_about(splits[0], (SAMPLES, Z, GRID, GRID, C), 1.0, 6.0, ((0, 8), (1, 32)))
    kernel = scatter_about(splits[1], (27, C, C), (27 * C) ** -0.5, 0.109375)
    cotangent = heavy_noise(splits[2], (SAMPLES, Z, GRID, GRID, C), 1.0, 6.0, ((0, 8), (1, 32)), (1, 4, 32, 2.75))
    return {"volume": volume, "kernel": kernel, "cotangent": cotangent}


def reference(volume, kernel, cotangent):
    factor = 1.0 / math.sqrt(SAMPLES * Z * GRID * GRID)

    def single(running, inputs):
        sample, upstream = inputs
        padded = jnp.pad(sample, ((1, 1), (1, 1), (1, 1), (0, 0)))
        padded_up = jnp.pad(upstream, ((1, 1), (1, 1), (1, 1), (0, 0)))
        flat_up = upstream.reshape(-1, C)
        output = jnp.zeros((Z * GRID * GRID, C), jnp.float32)
        backward = jnp.zeros((Z * GRID * GRID, C), jnp.float32)
        kernel_terms = []
        for tap_index in range(27):
            along_z = tap_index // 9
            along_y = tap_index // 3 % 3
            along_x = tap_index % 3
            window = padded[along_z:along_z + Z, along_y:along_y + GRID, along_x:along_x + GRID].reshape(-1, C)
            mirror = padded_up[2 - along_z:2 - along_z + Z, 2 - along_y:2 - along_y + GRID, 2 - along_x:2 - along_x + GRID].reshape(-1, C)
            output = output + jnp.dot(window, kernel[tap_index], preferred_element_type=jnp.float32)
            backward = backward + jnp.dot(mirror, kernel[tap_index].T, preferred_element_type=jnp.float32)
            kernel_terms.append(jnp.dot(flat_up.T, window, preferred_element_type=jnp.float32))
        shaped_out = output.reshape(Z, GRID, GRID, C).astype(jnp.bfloat16)
        shaped_back = backward.reshape(Z, GRID, GRID, C).astype(jnp.bfloat16)
        return (running + jnp.stack(kernel_terms, 1), (shaped_out, shaped_back))
    summed, (response, grad_volume) = lax.scan(single, jnp.zeros((C, 27, C), jnp.float32), (volume, cotangent))
    return (response, grad_volume, summed * factor)
```

```python
import functools
import math

import jax
import jax.numpy as jnp
from jax import lax
from jax.experimental import pallas as pl
from jax.experimental.pallas import tpu as pltpu
from jax.sharding import PartitionSpec as P

AXES = ("sample", "slab")
YS, CORES, XS, ZS = 4, 2, 4, 8
GRID, CELLS, C = 32, 1024, 128
PADDED = CELLS + 2 * GRID
F32, BF16 = jnp.float32, jnp.bfloat16
ANY = pl.BlockSpec(memory_space=pl.ANY)
VMEM = pl.BlockSpec(memory_space=pltpu.VMEM)
SMEM = pl.BlockSpec(memory_space=pltpu.SMEM)


def move(array, target):
    perm = []
    for y in range(YS):
        for core in range(CORES):
            for slab in range(XS * ZS):
                to = target(y, core, slab)
                if to is not None:
                    ty, tcore, tslab = to
                    perm.append(
                        ((y * CORES + core) * XS * ZS + slab, (ty * CORES + tcore) * XS * ZS + tslab)
                    )
    return lax.ppermute(array, AXES, perm)


def partner(y, core, slab):
    return y, core, slab ^ 1


def other(y, core, slab):
    to = slab - 1 if slab % 2 == 0 else slab + 1
    return (y, core, to) if 0 <= to < XS * ZS else None


def across_x(s):
    return lambda y, core, slab: (y, core, slab ^ (s * ZS))


def across_z(t):
    return lambda y, core, slab: (y, core, slab ^ (2 * t))


def across_y(s):
    return lambda y, core, slab: (y ^ s, core, slab)


def zero_edges(padded):
    padded[0:GRID] = jnp.zeros((GRID, C), BF16)
    padded[GRID + CELLS : PADDED] = jnp.zeros((GRID, C), BF16)


def row_order(place):
    r = lax.broadcasted_iota(jnp.int32, (C, C), 0)
    o = lax.broadcasted_iota(jnp.int32, (C, C), 1)
    half, s, t, j = r >> 6, (r >> 4) & 3, (r >> 2) & 3, r & 3
    wanted = ((place[1] ^ s) << 5) + ((place[2] ^ t) << 3) + ((place[0] ^ half) << 2) + j
    return jnp.where(o == wanted, 1.0, 0.0).astype(BF16)


def fill_rows(rows, order, cot):
    k = lax.broadcasted_iota(jnp.int32, (256, 256), 0)
    n = lax.broadcasted_iota(jnp.int32, (256, 256), 1)
    same = (k >> 5) == (n >> 5)
    left = jnp.where(same & (k == n + 1), 1.0, 0.0).astype(BF16)
    right = jnp.where(same & (k == n - 1), 1.0, 0.0).astype(BF16)
    for block in range(0, CELLS, 256):
        cells = slice(block, block + 256)
        turned = lax.dot_general(
            order, cot[cells], (((1,), (1,)), ((), ())), preferred_element_type=F32
        ).astype(BF16)
        rows[0:C, cells] = jnp.dot(turned, left, preferred_element_type=F32).astype(BF16)
        rows[C : 2 * C, cells] = turned
        rows[2 * C : 3 * C, cells] = jnp.dot(turned, right, preferred_element_type=F32).astype(BF16)


def product(rows, padded):
    wide = jnp.concatenate([padded[b * GRID : b * GRID + CELLS] for b in range(3)], axis=1)
    return jnp.dot(rows[...], wide, preferred_element_type=F32)


def write_pieces(total, keep, send):
    for s in range(4):
        for c in range(3):
            start = c * C + s * 16
            keep[s, c] = total[start : start + 16]
            send[s, c] = total[start + 64 : start + 80]


def centre_kernel(place, vol, cot, keep, send, padded, cots, rows, sems):
    copies = [
        pltpu.make_async_copy(cot, cots, sems.at[0]),
        pltpu.make_async_copy(vol, padded.at[pl.ds(GRID, CELLS)], sems.at[1]),
    ]
    for copy in copies:
        copy.start()
    zero_edges(padded)
    order = row_order(place)
    copies[0].wait()
    fill_rows(rows, order, cots)
    copies[1].wait()
    write_pieces(product(rows, padded), keep, send)


def side_kernel(place, vol, cot, near_vol, near_cot, keep, send, padded, cots, rows, sems):
    copies = [
        pltpu.make_async_copy(cot, cots.at[0], sems.at[0]),
        pltpu.make_async_copy(near_cot, cots.at[1], sems.at[1]),
        pltpu.make_async_copy(near_vol, padded.at[0, pl.ds(GRID, CELLS)], sems.at[2]),
        pltpu.make_async_copy(vol, padded.at[1, pl.ds(GRID, CELLS)], sems.at[3]),
    ]
    for copy in copies:
        copy.start()
    zero_edges(padded.at[0])
    zero_edges(padded.at[1])
    order = row_order(place)
    copies[0].wait()
    fill_rows(rows.at[0], order, cots.at[0])
    copies[1].wait()
    fill_rows(rows.at[1], order, cots.at[1])
    copies[2].wait()
    copies[3].wait()
    total = product(rows.at[0], padded.at[0]) + product(rows.at[1], padded.at[1])
    write_pieces(total, keep, send)


def conv_kernel(backward, weights, before, own, after, out, padded, weight, sems):
    planes = (after, own, before) if backward else (before, own, after)
    copies = [
        pltpu.make_async_copy(planes[a], padded.at[a, pl.ds(GRID, CELLS)], sems.at[a])
        for a in range(3)
    ] + [pltpu.make_async_copy(weights, weight, sems.at[3])]
    for copy in copies:
        copy.start()
    for a in range(3):
        zero_edges(padded.at[a])
    for copy in copies:
        copy.wait()
    pairs = [(0, 1), (2, 3), (4, 5), (6, 7), (8,)]

    @pl.loop(0, CELLS // 256)
    def _(block):
        start = pl.multiple_of(block * 256, 256)
        total = jnp.zeros((256, 3 * C), F32)
        for pair in pairs:
            left, right = [], []
            for ab in pair:
                a, b = ab // 3, ab % 3
                shift = (2 - b if backward else b) * GRID
                left.append(padded[a, pl.ds(pl.multiple_of(start + shift, GRID), 256), :])
                if backward:
                    right.append(
                        jnp.concatenate([weight[3 * ab + c] for c in range(3)], axis=0)
                    )
                else:
                    right.append(
                        jnp.concatenate([weight[3 * ab + c] for c in range(3)], axis=1)
                    )
            lhs = jnp.concatenate(left, axis=1)
            rhs = jnp.concatenate(right, axis=1 if backward else 0)
            dims = (((1,), (1 if backward else 0,)), ((), ()))
            total = total + lax.dot_general(lhs, rhs, dims, preferred_element_type=F32)
        low, mid, high = total[:, :C], total[:, C : 2 * C], total[:, 2 * C :]
        if backward:
            low, high = high, low
        x = lax.broadcasted_iota(jnp.int32, (256, C), 0) & (GRID - 1)
        low = jnp.where(x == 0, 0.0, pltpu.roll(low, 1, 0))
        high = jnp.where(x == GRID - 1, 0.0, pltpu.roll(high, 255, 0))
        out[pl.ds(start, 256), :] = (mid + low + high).astype(BF16)


PIECES = jax.ShapeDtypeStruct((4, 3, 16, 3 * C), F32)
PARAMS = pltpu.CompilerParams(vmem_limit_bytes=32 * 1024 * 1024)
TERM_FLOPS = 2 * 9 * CELLS * C * C


def centre(place, vol, cot):
    return pl.pallas_call(
        centre_kernel,
        out_shape=(PIECES, PIECES),
        in_specs=[SMEM, ANY, ANY],
        out_specs=(VMEM, VMEM),
        scratch_shapes=[
            pltpu.VMEM((PADDED, C), BF16),
            pltpu.VMEM((CELLS, C), BF16),
            pltpu.VMEM((3 * C, CELLS), BF16),
            pltpu.SemaphoreType.DMA((2,)),
        ],
        compiler_params=PARAMS,
        cost_estimate=pl.CostEstimate(flops=2 * TERM_FLOPS, bytes_accessed=4 << 20, transcendentals=0),
        name="centre",
    )(place, vol, cot)


def side(place, vol, cot, near_vol, near_cot):
    return pl.pallas_call(
        side_kernel,
        out_shape=(PIECES, PIECES),
        in_specs=[SMEM, ANY, ANY, ANY, ANY],
        out_specs=(VMEM, VMEM),
        scratch_shapes=[
            pltpu.VMEM((2, PADDED, C), BF16),
            pltpu.VMEM((2, CELLS, C), BF16),
            pltpu.VMEM((2, 3 * C, CELLS), BF16),
            pltpu.SemaphoreType.DMA((4,)),
        ],
        compiler_params=PARAMS,
        cost_estimate=pl.CostEstimate(flops=4 * TERM_FLOPS, bytes_accessed=8 << 20, transcendentals=0),
        name="side",
    )(place, vol, cot, near_vol, near_cot)


def conv(backward, weights, before, own, after):
    return pl.pallas_call(
        functools.partial(conv_kernel, backward),
        out_shape=jax.ShapeDtypeStruct((CELLS, C), BF16),
        in_specs=[ANY, ANY, ANY, ANY],
        out_specs=VMEM,
        scratch_shapes=[
            pltpu.VMEM((3, PADDED, C), BF16),
            pltpu.VMEM((27, C, C), BF16),
            pltpu.SemaphoreType.DMA((4,)),
        ],
        compiler_params=PARAMS,
        cost_estimate=pl.CostEstimate(flops=6 * TERM_FLOPS, bytes_accessed=8 << 20, transcendentals=0),
        name="grad_volume" if backward else "response",
    )(weights, before, own, after)


def reduce_x(keep, received):
    total = keep + received
    parts = [move(total[s], across_x(s)) for s in range(1, 4)]
    return total[0] + parts[0] + (parts[1] + parts[2])


def on_device(volume, kernel, cotangent):
    sample, slab = lax.axis_index("sample"), lax.axis_index("slab")
    core, z_odd = sample & 1, slab & 1
    place = jnp.stack([core, slab >> 3, (slab >> 1) & 3]).astype(jnp.int32)
    scale = 1.0 / math.sqrt(YS * CORES * XS * ZS * CELLS)
    vol, cot = volume.reshape(CELLS, C), cotangent.reshape(CELLS, C)

    partner_vol = move(vol, partner)
    other_cot = move(cot, other)
    partner_cot = move(cot, partner)
    other_vol = move(vol, other)
    swap = lambda y, c, s: (y, 1 - c, s)

    keep, send = centre(place, vol, cot)
    centre_sum = reduce_x(keep, move(send, swap))
    keep, send = side(place, vol, cot, partner_vol, other_cot)
    side_sum = reduce_x(keep, move(send, swap))

    even = z_odd == 0
    response = conv(
        False, kernel, jnp.where(even, other_vol, partner_vol), vol, jnp.where(even, partner_vol, other_vol)
    )
    grad_volume = conv(
        True, kernel, jnp.where(even, other_cot, partner_cot), cot, jnp.where(even, partner_cot, other_cot)
    )

    both = jnp.stack([centre_sum, side_sum]).reshape(2, 3, 4, 4, 3 * C)
    pieces = [both[:, :, t].reshape(24, 3 * C) for t in range(4)]
    parts = [move(pieces[t], across_z(t)) for t in range(1, 4)]
    total = pieces[0] + parts[0] + (parts[1] + parts[2])
    parts = [move(total, across_y(s)) for s in range(1, 4)]
    total = (total + parts[0]) + (parts[1] + parts[2])

    def first(y, c, s):
        p = s & 1
        return (y, c, s ^ 1) if c != p else (y, 1 - c, s)

    def second(y, c, s):
        return (y, 1 - c, s ^ 1) if c != (s & 1) else None

    one, two = move(total, first), move(total, second)
    same = core == z_odd
    from_even = jnp.where(same, jnp.where(even, total, one), jnp.where(even, one, two))
    from_odd = jnp.where(same, jnp.where(even, one, total), jnp.where(even, two, one))
    from_even, from_odd = from_even.reshape(2, 3, 4, 3, C), from_odd.reshape(2, 3, 4, 3, C)
    taps = jnp.stack([from_odd[1], from_even[0] + from_odd[0], from_even[1]])
    grad_kernel = (taps.transpose(2, 0, 3, 1, 4) * scale).reshape(4, 27, C)
    return (response.reshape(volume.shape), grad_volume.reshape(volume.shape), grad_kernel)


def solution(mesh):
    planes = P("sample", "slab", None, None, None)
    return jax.shard_map(
        on_device,
        mesh=mesh,
        in_specs=(planes, P(), planes),
        out_specs=(planes, planes, P("slab", None, None)),
        check_vma=False,
    )
```

```python
import functools
import math

import jax
import jax.numpy as jnp
from jax import lax
from jax.experimental import pallas as pl
from jax.experimental.pallas import tpu as pltpu
from jax.sharding import PartitionSpec as P

AXES = ("sample", "slab")
YS, CORES, XS, ZS = 4, 2, 4, 8
GRID, CELLS, C = 32, 1024, 128
PADDED = CELLS + 2 * GRID
F32, BF16 = jnp.float32, jnp.bfloat16
ANY = pl.BlockSpec(memory_space=pl.ANY)
HBM = pl.BlockSpec(memory_space=pltpu.HBM)
VMEM = pl.BlockSpec(memory_space=pltpu.VMEM)
SMEM = pl.BlockSpec(memory_space=pltpu.SMEM)


def move(array, target):
    perm = []
    for y in range(YS):
        for core in range(CORES):
            for slab in range(XS * ZS):
                to = target(y, core, slab)
                if to is not None:
                    ty, tcore, tslab = to
                    perm.append(
                        ((y * CORES + core) * XS * ZS + slab, (ty * CORES + tcore) * XS * ZS + tslab)
                    )
    return lax.ppermute(array, AXES, perm)


def partner(y, core, slab):
    return y, core, slab ^ 1


def other(y, core, slab):
    to = slab - 1 if slab % 2 == 0 else slab + 1
    return (y, core, to) if 0 <= to < XS * ZS else None


def across_x(s):
    return lambda y, core, slab: (y, core, slab ^ (s * ZS))


def across_y(s):
    return lambda y, core, slab: (y ^ s, core, slab)


def zero_edges(padded):
    padded[0:GRID] = jnp.zeros((GRID, C), BF16)
    padded[GRID + CELLS : PADDED] = jnp.zeros((GRID, C), BF16)


def row_order(place):
    r = lax.broadcasted_iota(jnp.int32, (C, C), 0)
    o = lax.broadcasted_iota(jnp.int32, (C, C), 1)
    half, s, t, j = r >> 6, (r >> 4) & 3, (r >> 2) & 3, r & 3
    wanted = ((place[1] ^ s) << 5) + ((place[2] ^ t) << 3) + ((place[0] ^ half) << 2) + j
    return jnp.where(o == wanted, 1.0, 0.0).astype(BF16)


def fill_rows(rows, order, cot):
    k = lax.broadcasted_iota(jnp.int32, (256, 256), 0)
    n = lax.broadcasted_iota(jnp.int32, (256, 256), 1)
    same = (k >> 5) == (n >> 5)
    left = jnp.where(same & (k == n + 1), 1.0, 0.0).astype(BF16)
    right = jnp.where(same & (k == n - 1), 1.0, 0.0).astype(BF16)
    for block in range(0, CELLS, 256):
        cells = slice(block, block + 256)
        turned = lax.dot_general(
            order, cot[cells], (((1,), (1,)), ((), ())), preferred_element_type=F32
        ).astype(BF16)
        rows[0:C, cells] = jnp.dot(turned, left, preferred_element_type=F32).astype(BF16)
        rows[C : 2 * C, cells] = turned
        rows[2 * C : 3 * C, cells] = jnp.dot(turned, right, preferred_element_type=F32).astype(BF16)


def product(rows, padded):
    wide = jnp.concatenate([padded[b * GRID : b * GRID + CELLS] for b in range(3)], axis=1)
    return jnp.dot(rows[...], wide, preferred_element_type=F32)


def write_pieces(total, keep, send, slot):
    for s in range(4):
        for c in range(3):
            start = c * C + s * 16
            keep[s, slot + c] = total[start : start + 16]
            send[s, slot + c] = total[start + 64 : start + 80]


def centre_kernel(place, vol, cot, keep, send, rows, padded, cots, sems):
    copies = [
        pltpu.make_async_copy(cot, cots, sems.at[0]),
        pltpu.make_async_copy(vol, padded.at[pl.ds(GRID, CELLS)], sems.at[1]),
    ]
    for copy in copies:
        copy.start()
    zero_edges(padded)
    order = row_order(place)
    copies[0].wait()
    fill_rows(rows, order, cots)
    copies[1].wait()
    write_pieces(product(rows, padded), keep, send, 0)


def side_kernel(
    place, vol, near_vol, near_cot, own_rows, keep0, send0, keep, send, padded, cots, rows, sems
):
    copies = [
        pltpu.make_async_copy(near_cot, cots, sems.at[0]),
        pltpu.make_async_copy(near_vol, padded.at[0, pl.ds(GRID, CELLS)], sems.at[1]),
        pltpu.make_async_copy(vol, padded.at[1, pl.ds(GRID, CELLS)], sems.at[2]),
    ]
    for copy in copies:
        copy.start()
    keep[:, 0:3] = keep0[...]
    send[:, 0:3] = send0[...]
    zero_edges(padded.at[0])
    zero_edges(padded.at[1])
    order = row_order(place)
    copies[0].wait()
    fill_rows(rows, order, cots)
    copies[1].wait()
    copies[2].wait()
    total = product(own_rows, padded.at[0]) + product(rows, padded.at[1])
    write_pieces(total, keep, send, 3)


def conv_kernel(backward, place, weights, partner_plane, own, other_plane, out, padded, weight, sems):
    after = 2 - 2 * place[3]
    partner_at = 2 - after if backward else after
    copies = [
        pltpu.make_async_copy(partner_plane, padded.at[partner_at, pl.ds(GRID, CELLS)], sems.at[0]),
        pltpu.make_async_copy(own, padded.at[1, pl.ds(GRID, CELLS)], sems.at[1]),
        pltpu.make_async_copy(other_plane, padded.at[2 - partner_at, pl.ds(GRID, CELLS)], sems.at[2]),
        pltpu.make_async_copy(weights, weight, sems.at[3]),
    ]
    for copy in copies:
        copy.start()
    for a in range(3):
        zero_edges(padded.at[a])
    for copy in copies:
        copy.wait()
    pairs = [tuple(range(9))]

    @pl.loop(0, CELLS // 1024)
    def _(block):
        start = pl.multiple_of(block * 1024, 1024)
        total = None
        for pair in pairs:
            left, right = [], []
            for ab in pair:
                a, b = ab // 3, ab % 3
                shift = (2 - b if backward else b) * GRID
                left.append(padded[a, pl.ds(pl.multiple_of(start + shift, GRID), 1024), :])
                right.append(
                    jnp.concatenate([weight[3 * ab + c] for c in range(3)], axis=0 if backward else 1)
                )
            lhs = jnp.concatenate(left, axis=1)
            rhs = jnp.concatenate(right, axis=1 if backward else 0)
            dims = (((1,), (1 if backward else 0,)), ((), ()))
            part = lax.dot_general(lhs, rhs, dims, preferred_element_type=F32)
            total = part if total is None else total + part
        low, mid, high = total[:, :C], total[:, C : 2 * C], total[:, 2 * C :]
        if backward:
            low, high = high, low
        x = lax.broadcasted_iota(jnp.int32, (1024, C), 0) & (GRID - 1)
        low = jnp.where(x == 0, 0.0, pltpu.roll(low, 1, 0))
        high = jnp.where(x == GRID - 1, 0.0, pltpu.roll(high, 1024 - 1, 0))
        out[pl.ds(start, 1024), :] = (mid + low + high).astype(BF16)


HALF = jax.ShapeDtypeStruct((4, 3, 16, 3 * C), F32)
WHOLE = jax.ShapeDtypeStruct((4, 6, 16, 3 * C), F32)
ROWS = jax.ShapeDtypeStruct((3 * C, CELLS), BF16)
COST = pl.CostEstimate(flops=1 << 20, bytes_accessed=1 << 16, transcendentals=0)
PARAMS = pltpu.CompilerParams(vmem_limit_bytes=32 * 1024 * 1024)


def centre(place, vol, cot):
    return pl.pallas_call(
        centre_kernel,
        out_shape=(HALF, HALF, ROWS),
        in_specs=[SMEM, HBM, HBM],
        out_specs=(VMEM, VMEM, VMEM),
        scratch_shapes=[
            pltpu.VMEM((PADDED, C), BF16),
            pltpu.VMEM((CELLS, C), BF16),
            pltpu.SemaphoreType.DMA((2,)),
        ],
        compiler_params=PARAMS,
        cost_estimate=COST,
        name="centre",
    )(place, vol, cot)


def side(place, vol, near_vol, near_cot, rows, keep, send):
    return pl.pallas_call(
        side_kernel,
        out_shape=(WHOLE, WHOLE),
        in_specs=[SMEM, HBM, ANY, ANY, VMEM, VMEM, VMEM],
        out_specs=(VMEM, VMEM),
        scratch_shapes=[
            pltpu.VMEM((2, PADDED, C), BF16),
            pltpu.VMEM((CELLS, C), BF16),
            pltpu.VMEM((3 * C, CELLS), BF16),
            pltpu.SemaphoreType.DMA((3,)),
        ],
        compiler_params=PARAMS,
        cost_estimate=COST,
        name="side",
    )(place, vol, near_vol, near_cot, rows, keep, send)


def conv(backward, place, weights, partner_plane, own, other_plane):
    return pl.pallas_call(
        functools.partial(conv_kernel, backward),
        out_shape=jax.ShapeDtypeStruct((CELLS, C), BF16),
        in_specs=[SMEM, ANY, ANY, HBM, ANY],
        out_specs=VMEM,
        scratch_shapes=[
            pltpu.VMEM((3, PADDED, C), BF16),
            pltpu.VMEM((27, C, C), BF16),
            pltpu.SemaphoreType.DMA((4,)),
        ],
        compiler_params=PARAMS,
        cost_estimate=COST,
        name="grad_volume" if backward else "response",
    )(place, weights, partner_plane, own, other_plane)


def after(value, *earlier):
    return lax.optimization_barrier((value, *earlier))[0]


def on_device(volume, kernel, cotangent):
    sample, slab = lax.axis_index("sample"), lax.axis_index("slab")
    core, z_odd = sample & 1, slab & 1
    place = jnp.stack([core, slab >> 3, (slab >> 1) & 3, z_odd]).astype(jnp.int32)
    scale = 1.0 / math.sqrt(YS * CORES * XS * ZS * CELLS)
    vol, cot = volume.reshape(CELLS, C), cotangent.reshape(CELLS, C)
    swap = lambda y, c, s: (y, 1 - c, s)

    other_cot = move(cot, other)
    other_vol = move(vol, other)
    partner_vol = move(vol, partner)
    partner_cot = move(cot, partner)
    keep, send, rows = centre(place, vol, cot)
    keep, send = side(place, vol, partner_vol, other_cot, rows, keep, send)
    total = keep + move(after(send, other_vol, partner_cot), swap)

    away = total[1:]
    peak = jnp.max(jnp.abs(away), axis=(1, 3), keepdims=True)
    power = jnp.clip(jnp.ceil(jnp.log2(peak)), -100.0, 100.0)
    scaled = (away * jnp.exp2(-power)).astype(jnp.float16)
    powers = jnp.broadcast_to(power, (3, 1, 16, 3 * C)).astype(jnp.float16)
    packed = jnp.concatenate([scaled, powers], axis=1)
    parts = [move(packed[s - 1], across_x(s)) for s in range(1, 4)]
    parts = [p[:6].astype(F32) * jnp.exp2(p[6:].astype(F32)) for p in parts]
    grad_volume = conv(True, after(place, total), kernel, partner_cot, cot, other_cot)
    total = total[0] + parts[0] + (parts[1] + parts[2])
    total = after(total, grad_volume)

    pieces = [total.reshape(6, 4, 4, 3 * C)[:, t].reshape(24, 3 * C) for t in range(4)]

    def to_owner(t):
        return lambda y, c, s: (y, s & 1, ((s ^ (2 * t)) & ~1) | c)

    parts = [move(pieces[t], to_owner(t)) for t in range(4)]
    response = conv(False, after(place, total), kernel, partner_vol, vol, other_vol)
    total = (parts[0] + parts[1]) + (parts[2] + parts[3])
    total = after(total, response)

    for s in (1, 3):
        total = total + move(total, across_y(s))
    twin = move(total, swap)
    from_even = jnp.where(core == 0, total, twin).reshape(2, 3, 4, 3, C)
    from_odd = jnp.where(core == 0, twin, total).reshape(2, 3, 4, 3, C)
    taps = jnp.stack([from_odd[1], from_even[0] + from_odd[0], from_even[1]])
    grad_kernel = (taps.transpose(2, 0, 3, 1, 4) * scale).reshape(4, 27, C)
    return (response.reshape(volume.shape), grad_volume.reshape(volume.shape), grad_kernel)


def solution(mesh):
    planes = P("sample", "slab", None, None, None)
    return jax.shard_map(
        on_device,
        mesh=mesh,
        in_specs=(planes, P(), planes),
        out_specs=(planes, planes, P("slab", None, None)),
        check_vma=False,
    )
```

```python
import functools
import math

import jax
import jax.numpy as jnp
from jax import lax
from jax.experimental import pallas as pl
from jax.experimental.pallas import tpu as pltpu
from jax.sharding import PartitionSpec as P

AXES = ("sample", "slab")
YS, CORES, XS, ZS = 4, 2, 4, 8
GRID, CELLS, C = 32, 1024, 128
PADDED = CELLS + 2 * GRID
F32, BF16 = jnp.float32, jnp.bfloat16
ANY = pl.BlockSpec(memory_space=pl.ANY)
HBM = pl.BlockSpec(memory_space=pltpu.HBM)
VMEM = pl.BlockSpec(memory_space=pltpu.VMEM)
SMEM = pl.BlockSpec(memory_space=pltpu.SMEM)


def move(array, target):
    perm = []
    for y in range(YS):
        for core in range(CORES):
            for slab in range(XS * ZS):
                to = target(y, core, slab)
                if to is not None:
                    ty, tcore, tslab = to
                    perm.append(
                        ((y * CORES + core) * XS * ZS + slab, (ty * CORES + tcore) * XS * ZS + tslab)
                    )
    return lax.ppermute(array, AXES, perm)


def partner(y, core, slab):
    return y, core, slab ^ 1


def other(y, core, slab):
    to = slab - 1 if slab % 2 == 0 else slab + 1
    return (y, core, to) if 0 <= to < XS * ZS else None


def across_x(s):
    return lambda y, core, slab: (y, core, slab ^ (s * ZS))


def across_y(s):
    return lambda y, core, slab: (y ^ s, core, slab)


def zero_edges(padded):
    padded[0:GRID] = jnp.zeros((GRID, C), BF16)
    padded[GRID + CELLS : PADDED] = jnp.zeros((GRID, C), BF16)


def row_order(place):
    r = lax.broadcasted_iota(jnp.int32, (C, C), 0)
    o = lax.broadcasted_iota(jnp.int32, (C, C), 1)
    half, s, t, j = r >> 6, (r >> 4) & 3, (r >> 2) & 3, r & 3
    wanted = ((place[1] ^ s) << 5) + ((place[2] ^ t) << 3) + ((place[0] ^ half) << 2) + j
    return jnp.where(o == wanted, 1.0, 0.0).astype(BF16)


def fill_rows(rows, order, cot):
    k = lax.broadcasted_iota(jnp.int32, (256, 256), 0)
    n = lax.broadcasted_iota(jnp.int32, (256, 256), 1)
    same = (k >> 5) == (n >> 5)
    left = jnp.where(same & (k == n + 1), 1.0, 0.0).astype(BF16)
    right = jnp.where(same & (k == n - 1), 1.0, 0.0).astype(BF16)
    for block in range(0, CELLS, 256):
        cells = slice(block, block + 256)
        turned = lax.dot_general(
            order, cot[cells], (((1,), (1,)), ((), ())), preferred_element_type=F32
        ).astype(BF16)
        rows[0:C, cells] = jnp.dot(turned, left, preferred_element_type=F32).astype(BF16)
        rows[C : 2 * C, cells] = turned
        rows[2 * C : 3 * C, cells] = jnp.dot(turned, right, preferred_element_type=F32).astype(BF16)


def product(rows, padded):
    wide = jnp.concatenate([padded[b * GRID : b * GRID + CELLS] for b in range(3)], axis=1)
    return jnp.dot(rows[...], wide, preferred_element_type=F32)


def write_pieces(total, keep, send, slot):
    for s in range(4):
        for c in range(3):
            start = c * C + s * 16
            lanes = slice((slot + c) * 3 * C, (slot + c + 1) * 3 * C)
            keep[s, :, lanes] = total[start : start + 16]
            send[s, :, lanes] = total[start + 64 : start + 80]


def centre_kernel(place, vol, cot, keep, send, rows, padded, cots, sems):
    copies = [
        pltpu.make_async_copy(cot, cots, sems.at[0]),
        pltpu.make_async_copy(vol, padded.at[pl.ds(GRID, CELLS)], sems.at[1]),
    ]
    for copy in copies:
        copy.start()
    zero_edges(padded)
    order = row_order(place)
    copies[0].wait()
    fill_rows(rows, order, cots)
    copies[1].wait()
    write_pieces(product(rows, padded), keep, send, 0)


def side_kernel(
    place, vol, near_vol, near_cot, own_rows, keep0, send0, keep, send, padded, cots, rows, sems
):
    copies = [
        pltpu.make_async_copy(near_cot, cots, sems.at[0]),
        pltpu.make_async_copy(near_vol, padded.at[0, pl.ds(GRID, CELLS)], sems.at[1]),
        pltpu.make_async_copy(vol, padded.at[1, pl.ds(GRID, CELLS)], sems.at[2]),
    ]
    for copy in copies:
        copy.start()
    keep[:, :, 0 : 9 * C] = keep0[...]
    send[:, :, 0 : 9 * C] = send0[...]
    zero_edges(padded.at[0])
    zero_edges(padded.at[1])
    order = row_order(place)
    copies[0].wait()
    fill_rows(rows, order, cots)
    copies[1].wait()
    copies[2].wait()
    total = product(own_rows, padded.at[0]) + product(rows, padded.at[1])
    write_pieces(total, keep, send, 3)


def conv_kernel(backward, place, weights, partner_plane, own, other_plane, out, padded, weight, sems):
    after = 2 - 2 * place[3]
    partner_at = 2 - after if backward else after
    copies = [
        pltpu.make_async_copy(partner_plane, padded.at[partner_at, pl.ds(GRID, CELLS)], sems.at[0]),
        pltpu.make_async_copy(own, padded.at[1, pl.ds(GRID, CELLS)], sems.at[1]),
        pltpu.make_async_copy(other_plane, padded.at[2 - partner_at, pl.ds(GRID, CELLS)], sems.at[2]),
        pltpu.make_async_copy(weights, weight, sems.at[3]),
    ]
    for copy in copies:
        copy.start()
    for a in range(3):
        zero_edges(padded.at[a])
    for copy in copies:
        copy.wait()
    pairs = [tuple(range(9))]

    @pl.loop(0, CELLS // 1024)
    def _(block):
        start = pl.multiple_of(block * 1024, 1024)
        total = None
        for pair in pairs:
            left, right = [], []
            for ab in pair:
                a, b = ab // 3, ab % 3
                shift = (2 - b if backward else b) * GRID
                left.append(padded[a, pl.ds(pl.multiple_of(start + shift, GRID), 1024), :])
                right.append(
                    jnp.concatenate([weight[3 * ab + c] for c in range(3)], axis=0 if backward else 1)
                )
            lhs = jnp.concatenate(left, axis=1)
            rhs = jnp.concatenate(right, axis=1 if backward else 0)
            dims = (((1,), (1 if backward else 0,)), ((), ()))
            part = lax.dot_general(lhs, rhs, dims, preferred_element_type=F32)
            total = part if total is None else total + part
        low, mid, high = total[:, :C], total[:, C : 2 * C], total[:, 2 * C :]
        if backward:
            low, high = high, low
        x = lax.broadcasted_iota(jnp.int32, (1024, C), 0) & (GRID - 1)
        low = jnp.where(x == 0, 0.0, pltpu.roll(low, 1, 0))
        high = jnp.where(x == GRID - 1, 0.0, pltpu.roll(high, 1024 - 1, 0))
        out[pl.ds(start, 1024), :] = (mid + low + high).astype(BF16)


HALF = jax.ShapeDtypeStruct((4, 16, 9 * C), F32)
WHOLE = jax.ShapeDtypeStruct((4, 16, 18 * C), F32)
ROWS = jax.ShapeDtypeStruct((3 * C, CELLS), BF16)
COST = pl.CostEstimate(flops=1 << 20, bytes_accessed=1 << 16, transcendentals=0)
PARAMS = pltpu.CompilerParams(vmem_limit_bytes=32 * 1024 * 1024)


def centre(place, vol, cot):
    return pl.pallas_call(
        centre_kernel,
        out_shape=(HALF, HALF, ROWS),
        in_specs=[SMEM, HBM, HBM],
        out_specs=(VMEM, VMEM, VMEM),
        scratch_shapes=[
            pltpu.VMEM((PADDED, C), BF16),
            pltpu.VMEM((CELLS, C), BF16),
            pltpu.SemaphoreType.DMA((2,)),
        ],
        compiler_params=PARAMS,
        cost_estimate=COST,
        name="centre",
    )(place, vol, cot)


def side(place, vol, near_vol, near_cot, rows, keep, send):
    return pl.pallas_call(
        side_kernel,
        out_shape=(WHOLE, WHOLE),
        in_specs=[SMEM, HBM, ANY, ANY, VMEM, VMEM, VMEM],
        out_specs=(VMEM, VMEM),
        scratch_shapes=[
            pltpu.VMEM((2, PADDED, C), BF16),
            pltpu.VMEM((CELLS, C), BF16),
            pltpu.VMEM((3 * C, CELLS), BF16),
            pltpu.SemaphoreType.DMA((3,)),
        ],
        compiler_params=PARAMS,
        cost_estimate=COST,
        name="side",
    )(place, vol, near_vol, near_cot, rows, keep, send)


def conv(backward, place, weights, partner_plane, own, other_plane):
    return pl.pallas_call(
        functools.partial(conv_kernel, backward),
        out_shape=jax.ShapeDtypeStruct((CELLS, C), BF16),
        in_specs=[SMEM, ANY, ANY, HBM, ANY],
        out_specs=VMEM,
        scratch_shapes=[
            pltpu.VMEM((3, PADDED, C), BF16),
            pltpu.VMEM((27, C, C), BF16),
            pltpu.SemaphoreType.DMA((4,)),
        ],
        compiler_params=PARAMS,
        cost_estimate=COST,
        name="grad_volume" if backward else "response",
    )(place, weights, partner_plane, own, other_plane)


def after(value, *earlier):
    return lax.optimization_barrier((value, *earlier))[0]


def on_device(volume, kernel, cotangent):
    sample, slab = lax.axis_index("sample"), lax.axis_index("slab")
    core, z_odd = sample & 1, slab & 1
    place = jnp.stack([core, slab >> 3, (slab >> 1) & 3, z_odd]).astype(jnp.int32)
    scale = 1.0 / math.sqrt(YS * CORES * XS * ZS * CELLS)
    vol, cot = volume.reshape(CELLS, C), cotangent.reshape(CELLS, C)
    swap = lambda y, c, s: (y, 1 - c, s)

    other_cot = move(cot, other)
    other_vol = move(vol, other)
    partner_vol = move(vol, partner)
    partner_cot = move(cot, partner)
    keep, send, rows = centre(place, vol, cot)
    keep, send = side(place, vol, partner_vol, other_cot, rows, keep, send)
    total = keep + move(after(send, other_vol, partner_cot), swap)

    away = total[1:]
    peak = jnp.max(jnp.abs(away), axis=2, keepdims=True)
    power = jnp.clip(jnp.ceil(jnp.log2(peak)), -126.0, 100.0)
    scaled = (away * jnp.exp2(-power)).astype(jnp.float16)
    powers = jnp.broadcast_to(power, (3, 16, C)).astype(jnp.float16)
    packed = jnp.concatenate([scaled, powers], axis=2)
    parts = [move(packed[s - 1], across_x(s)) for s in range(1, 4)]
    parts = [p[:, : 18 * C].astype(F32) * jnp.exp2(p[:, 18 * C : 18 * C + 1].astype(F32)) for p in parts]
    grad_volume = conv(True, after(place, total), kernel, partner_cot, cot, other_cot)
    total = total[0] + parts[0] + (parts[1] + parts[2])
    total = after(total, grad_volume)

    pieces = [total[4 * t : 4 * t + 4] for t in range(4)]

    def to_owner(t):
        return lambda y, c, s: (y, s & 1, ((s ^ (2 * t)) & ~1) | c)

    parts = [move(pieces[t], to_owner(t)) for t in range(4)]
    response = conv(False, after(place, total), kernel, partner_vol, vol, other_vol)
    total = (parts[0] + parts[1]) + (parts[2] + parts[3])
    total = after(total, response)

    total = total + move(total, across_y(1))
    total = total + move(total, across_y(3))
    twin = move(total, swap)
    from_even = jnp.where(core == 0, total, twin).reshape(4, 2, 3, 3, C)
    from_odd = jnp.where(core == 0, twin, total).reshape(4, 2, 3, 3, C)
    taps = jnp.stack([from_odd[:, 1], from_even[:, 0] + from_odd[:, 0], from_even[:, 1]], axis=1)
    grad_kernel = (taps.transpose(0, 1, 3, 2, 4) * scale).reshape(4, 27, C)
    return (response.reshape(volume.shape), grad_volume.reshape(volume.shape), grad_kernel)


def solution(mesh):
    planes = P("sample", "slab", None, None, None)
    return jax.shard_map(
        on_device,
        mesh=mesh,
        in_specs=(planes, P(), planes),
        out_specs=(planes, planes, P("slab", None, None)),
        check_vma=False,
    )
```
